128 devices in a mesh: dp: 16 (over z, x_lo, core), seq: 8 (over y, x_hi).
Axes of the slice: x: 4 (x_hi: 2, x_lo: 2; x = x_hi * 2 + x_lo), y: 4, z: 4, core: 2. Of those that a mesh axis runs over, the one named last changes fastest.
Arguments:
- stream_one: bfloat16 [16, 2048, 2048], P('dp', 'seq'), may hold values from -6 to 6
- stream_two: bfloat16 [16, 2048, 2048], P('dp', 'seq'), may hold values from -300 to 300
- cotan_one: bfloat16 [16, 2048, 2048], P('dp', 'seq'), may hold values from -6 to 6
- cotan_two: bfloat16 [16, 2048, 2048], P('dp', 'seq'), may hold values from -6 to 6
- first_key: int32 [16, 16], P('dp'), may hold values from 0 to 1920, as said below
- w_query: bfloat16 [2048, 1024], P('dp'), may hold values from -1 to 1
- w_key: bfloat16 [2048, 1024], P('dp'), may hold values from -4 to 4
- w_value: bfloat16 [2048, 1024], P('dp'), may hold values from -0.125 to 0.125
- w_out: bfloat16 [1024, 2048], P('dp'), may hold values from -0.1875 to 0.1875
Outputs:
- input_one: bfloat16 [16, 2048, 2048], P('dp', 'seq')
- grad_two: bfloat16 [16, 2048, 2048], P('dp', 'seq')
- grad_query: float32 [2048, 1024], P('dp')
- grad_key: float32 [2048, 1024], P('dp')
- grad_value: float32 [2048, 1024], P('dp')
- grad_out: float32 [1024, 2048], P('dp')
The draws below stay inside these ranges and needn't reach their ends.
Inputs may be any that keep to these rules, and one draw needn't show every extreme that they name: first_key[s, b] is the earliest key position visible to queries b * 128 to (b + 1) * 128 - 1 of sequence s, never after b * 128.
All inputs are finite; a program needn't handle non-finite values.
Results may differ from the reference program's by a relative error of at most 0.03.
The reference program's roundings to bfloat16 on the way (of `attended`, `attended_grad`, `value_grad`, `score_grad` and `span_terms`) count: a program that leaves them out, or rounds other values in their place, can miss the bound.
Values may be sent and summed in bfloat16 or wider, within the bound.
No kernel may reach another device: no remote copies, remote signals or barrier semaphores. Data moves between devices by JAX's collectives and lax.ppermute only.
A program may use at most 128 MiB of HBM per device.

```python
import math
import jax
import jax.numpy as jnp
from jax import lax

D = 2048
HEADS = 8
HD = 128
TD = 256
QBLK = 128
HQ = 1024
LEN = 2048
SEQS = 16
NQB = 16
N_SEQ = 8


def shared_projection(key):
    drawn = jax.random.normal(key, (D, HEADS * HD), jnp.float32)
    return jnp.clip(drawn, -6.0, 6.0) * D ** (-0.5)


def draw_w_query(key, part):
    shared = shared_projection(key)
    return shared.astype(jnp.bfloat16)


def draw_w_key(key, part):
    key = jax.random.fold_in(key, 6)
    own_key = jax.random.fold_in(key, 0)
    own_part = jnp.clip(jax.random.normal(own_key, (D, HEADS * HD), jnp.float32), -6.0, 6.0) * D ** (-0.5)
    return own_part.astype(jnp.bfloat16)


def draw_stream_two(key, part):
    key = jax.random.fold_in(key, 3)
    value_key, row_key, column_key = jax.random.split(key, 3)
    column_scale = jnp.exp(jax.random.uniform(column_key, (1, 1, D), jnp.float32, math.log(0.3), math.log(3.0)))
    rows_scale = jnp.exp(jax.random.uniform(row_key, (SEQS, LEN, 1), jnp.float32) * math.log(10.0))
    values = jnp.clip(jax.random.normal(value_key, (SEQS, LEN, D), jnp.float32), -6.0, 6.0)
    return (values * rows_scale * column_scale).astype(jnp.bfloat16)


def draw_first_key(key, part):
    key = jax.random.fold_in(key, 9)
    value_key, zero_key = jax.random.split(key)
    starts = jnp.arange(NQB, dtype=jnp.int32) * QBLK
    drawn_values = jax.random.randint(value_key, (SEQS, NQB), 0, 1 << 20)
    picked = drawn_values % (starts[None, :] + 1)
    zeroed = jax.random.randint(zero_key, (SEQS, NQB), 0, 2)
    result = jnp.where(zeroed == 1, 0, picked).astype(jnp.int32)
    seq_index = jnp.arange(SEQS, dtype=jnp.int32)[:, None]
    block_index = jnp.arange(NQB, dtype=jnp.int32)[None, :]
    pinned = (seq_index == 0) & (block_index == NQB - 1)
    return jnp.where(pinned, starts[None, :], result).astype(jnp.int32)


def block_levels(key, shape, shards, least, high):
    def one(axis_at, blocks):
        draws = jax.random.uniform(jax.random.fold_in(jax.random.fold_in(key, 6), axis_at), (blocks,), jnp.float32, least / len(shards), high / len(shards))
        return jnp.repeat(jnp.exp(draws), shape[axis_at] // blocks).reshape((-1,) + (1,) * (len(shape) - axis_at - 1))

    factor_of = one(*shards[0])
    for cut in shards[1:]:
        factor_of = factor_of * one(*cut)
    return factor_of


def centred(stream_key, extent, width, limit, cuts=(), kind=jnp.bfloat16):
    array = jax.random.normal(stream_key, extent, jnp.float32) * width
    if len(cuts) > 0:
        array = block_levels(stream_key, extent, cuts, -0.22, 0.18) * array
    return jnp.clip(array, min=-limit, max=limit).astype(kind)


def setup_inputs(seed: int = 0) -> dict:
    key_of = jax.random.split(jax.random.key(seed), 10)
    stream_one = centred(key_of[0], (SEQS, LEN, D), 1.0, 6.0, ((0, 16), (1, 8)))
    stream_two = draw_stream_two(jax.random.fold_in(key_of[9], 71), 0)
    cotan_one = centred(key_of[2], (SEQS, LEN, D), 1.0, 6.0, ((0, 16), (1, 8)))
    cotan_two = centred(key_of[3], (SEQS, LEN, D), 1.0, 6.0, ((0, 16), (1, 8)))
    first_key = draw_first_key(jax.random.fold_in(key_of[9], 71), 0)
    w_query = draw_w_query(jax.random.fold_in(key_of[9], 71), 0)
    w_key = draw_w_key(jax.random.fold_in(key_of[9], 71), 0)
    w_value = centred(key_of[7], (D, HQ), D ** -0.5, 0.125, ((0, 16),))
    w_out = centred(key_of[8], (HQ, D), HQ ** -0.5, 0.1875, ((0, 16),))
    return {"stream_one": stream_one, "stream_two": stream_two, "cotan_one": cotan_one, "cotan_two": cotan_two, "first_key": first_key, "w_query": w_query, "w_key": w_key, "w_value": w_value, "w_out": w_out}


eps = 1e-06

def rms_rows(stream):
    values = stream.astype(jnp.float32)
    inverse = lax.rsqrt(lax.optimization_barrier(jnp.mean(values * values, axis=-1, keepdims=True)) + eps)
    return (values * inverse, inverse)

def rounded(values):
    return lax.optimization_barrier(values.astype(jnp.bfloat16)).astype(jnp.float32)

def reference(stream_one, stream_two, cotan_one, cotan_two, first_key, w_query, w_key, w_value, w_out):
    normed, inverse = rms_rows(stream_two)
    normed_low = normed.astype(jnp.bfloat16)
    flat_normed = normed_low.reshape(SEQS * LEN, D)

    def project(weight):
        product = jnp.dot(flat_normed, weight, preferred_element_type=jnp.float32)
        return product.astype(jnp.bfloat16).reshape(SEQS, LEN, HEADS, HD)
    query_heads = project(w_query)
    key_heads = project(w_key)
    value_heads = project(w_value)
    positions = jnp.arange(LEN, dtype=jnp.int32)
    earliest = jnp.broadcast_to(first_key[:, :, None], (SEQS, NQB, QBLK)).reshape(SEQS, LEN)
    visible = (positions[None, None, :] <= positions[None, :, None]) & (positions[None, None, :] >= earliest[:, :, None])
    softmax_scale = HD ** (-0.5)

    def weights_of(head_index):
        query_part = query_heads[:, :, head_index].astype(jnp.float32)
        key_part = key_heads[:, :, head_index].astype(jnp.float32)
        scores = jnp.einsum('sqd,skd->sqk', query_part, key_part) * softmax_scale
        scores = jnp.where(visible, scores, -1e+30)
        return jax.nn.softmax(scores, axis=-1)

    def forward_head(head_index):
        probabilities = rounded(weights_of(head_index))
        value_part = value_heads[:, :, head_index].astype(jnp.float32)
        return jnp.einsum('sqk,skd->sqd', probabilities, value_part).astype(jnp.bfloat16)
    attended = lax.map(forward_head, jnp.arange(HEADS))
    attended_heads = jnp.transpose(attended, (1, 2, 0, 3))
    attended_flat = attended_heads.reshape(SEQS * LEN, HEADS * HD)
    mixed_rows = jnp.dot(attended_flat, w_out, preferred_element_type=jnp.float32)
    input_one = (stream_one.astype(jnp.float32).reshape(SEQS * LEN, D) - mixed_rows).astype(jnp.bfloat16).reshape(SEQS, LEN, D)
    flat_cotan = cotan_one.reshape(SEQS * LEN, D)
    attended_grad = jnp.dot(flat_cotan, w_out.T, preferred_element_type=jnp.float32).astype(jnp.bfloat16)
    grad_heads = attended_grad.reshape(SEQS, LEN, HEADS, HD)

    def backward_head(head_index):
        probabilities = weights_of(head_index)
        probs_low = rounded(probabilities)
        grad_part = grad_heads[:, :, head_index].astype(jnp.float32)
        value_part = value_heads[:, :, head_index].astype(jnp.float32)
        query_part = query_heads[:, :, head_index].astype(jnp.float32)
        key_part = key_heads[:, :, head_index].astype(jnp.float32)
        out_part = attended_heads[:, :, head_index].astype(jnp.float32)
        value_grad = jnp.einsum('sqk,sqd->skd', probs_low, grad_part).astype(jnp.bfloat16)
        grad_probs = jnp.einsum('sqd,skd->sqk', grad_part, value_part)
        row_dots = lax.optimization_barrier(jnp.sum(grad_part * out_part, axis=-1, keepdims=True))
        score_grad = rounded(probabilities * (grad_probs - row_dots))
        query_grad = (jnp.einsum('sqk,skd->sqd', score_grad, key_part) * softmax_scale).astype(jnp.bfloat16)
        key_grad = (jnp.einsum('sqk,sqd->skd', score_grad, query_part) * softmax_scale).astype(jnp.bfloat16)
        return (query_grad, key_grad, value_grad)
    query_grads, key_grads, value_grads = lax.map(backward_head, jnp.arange(HEADS))

    def to_rows(stacked):
        return jnp.transpose(stacked, (1, 2, 0, 3)).reshape(SEQS * LEN, HEADS * HD)
    query_flat = to_rows(query_grads)
    key_flat = to_rows(key_grads)
    value_flat = to_rows(value_grads)
    normed_grad = jnp.dot(query_flat, w_query.T, preferred_element_type=jnp.float32)
    normed_grad = normed_grad + jnp.dot(key_flat, w_key.T, preferred_element_type=jnp.float32)
    normed_grad = normed_grad + jnp.dot(value_flat, w_value.T, preferred_element_type=jnp.float32)
    normed_flat = normed.reshape(SEQS * LEN, D)
    inverse_flat = inverse.reshape(SEQS * LEN, 1)
    correction = lax.optimization_barrier(jnp.mean(normed_grad * normed_flat, axis=-1, keepdims=True))
    grad_two = cotan_two.astype(jnp.float32).reshape(SEQS * LEN, D) + inverse_flat * (normed_grad - normed_flat * correction)
    grad_two = grad_two.astype(jnp.bfloat16).reshape(SEQS, LEN, D)

    def spanned(values):
        return values.reshape(SEQS * N_SEQ, TD, values.shape[-1])

    def add_span(totals, pieces):
        normed_piece, query_piece, key_piece, value_piece, attended_piece, cotan_piece = pieces
        span_terms = (jnp.dot(normed_piece.T, query_piece, preferred_element_type=jnp.float32).astype(jnp.bfloat16), jnp.dot(normed_piece.T, key_piece, preferred_element_type=jnp.float32).astype(jnp.bfloat16), jnp.dot(normed_piece.T, value_piece, preferred_element_type=jnp.float32).astype(jnp.bfloat16), jnp.dot(attended_piece.T, cotan_piece, preferred_element_type=jnp.float32).astype(jnp.bfloat16))
        span_terms = lax.optimization_barrier(span_terms)
        return (tuple((partial_sum + term_piece.astype(jnp.float32) for partial_sum, term_piece in zip(totals, span_terms))), None)
    initial = (jnp.zeros((D, HEADS * HD), jnp.float32), jnp.zeros((D, HEADS * HD), jnp.float32), jnp.zeros((D, HEADS * HD), jnp.float32), jnp.zeros((HEADS * HD, D), jnp.float32))
    totals, _ = lax.scan(add_span, initial, (spanned(flat_normed), spanned(query_flat), spanned(key_flat), spanned(value_flat), spanned(attended_flat), spanned(flat_cotan)))
    return (input_one, grad_two, totals[0], totals[1], totals[2], totals[3])
```

```python
import jax
import jax.numpy as jnp
from jax import lax
from jax.experimental import pallas as pl
from jax.experimental.pallas import tpu as pltpu
from jax.sharding import PartitionSpec as P

HEADS = 8
HD = 128
QBLK = 128
EPS = 1e-06
SCALE = HD ** (-0.5)
AXES = ("dp", "seq")
BF = jnp.bfloat16
F32 = jnp.float32
TB = 256
LEN = 2048
D = 2048

COORDS = [
    (z, xl, c, y, xh)
    for z in range(4)
    for xl in range(2)
    for c in range(2)
    for y in range(4)
    for xh in range(2)
]


def flat(z, xl, c, y, xh):
    return (z * 4 + xl * 2 + c) * 8 + y * 2 + xh


def perm(move):
    return [(flat(*at), flat(*move(*at))) for at in COORDS]


def x_step(step):
    def move(z, xl, c, y, xh):
        x = (xh * 2 + xl + step) % 4
        return (z, x % 2, c, y, x // 2)

    return move


SWITCH = perm(lambda z, xl, c, y, xh: (z, xl, xh, y, c))
CORE = perm(lambda z, xl, c, y, xh: (z, xl, 1 - c, y, xh))
HALF = perm(lambda z, xl, c, y, xh: (z, xl, c, y, 1 - xh))
Y_UP = perm(lambda z, xl, c, y, xh: (z, xl, c, (y + 1) % 4, xh))
Y_DOWN = perm(lambda z, xl, c, y, xh: (z, xl, c, (y - 1) % 4, xh))
Z_UP = perm(lambda z, xl, c, y, xh: ((z + 1) % 4, xl, c, y, xh))
Z_DOWN = perm(lambda z, xl, c, y, xh: ((z - 1) % 4, xl, c, y, xh))
X_UP = perm(x_step(1))
X_DOWN = perm(x_step(-1))
GROUP_YC = [
    [flat(z, xl, c, y, xh) for y in range(4) for c in range(2)]
    for z in range(4)
    for xl in range(2)
    for xh in range(2)
]
GROUP_ZX = [
    [flat(z, xl, c, y, xh) for z in range(4) for xl in range(2) for xh in range(2)]
    for y in range(4)
    for c in range(2)
]


def send(value, pairs):
    return lax.ppermute(value, AXES, pairs)


def ring4(piece, up, down, axis):
    from_below = send(piece, up)
    from_above = send(piece, down)
    half = piece.shape[axis] // 2
    low = lax.slice_in_dim(from_below, 0, half, axis=axis)
    high = lax.slice_in_dim(from_above, half, 2 * half, axis=axis)
    far_low = send(low, up)
    far_high = send(high, down)
    return (
        jnp.concatenate([piece, from_below], axis=axis),
        jnp.concatenate([from_above, far_low, far_high], axis=axis),
    )


RELATIVE = ((0, -1), (1, 2))


def dot(a, b, dims=((1,), (0,))):
    return lax.dot_general(a, b, (dims, ((), ())), preferred_element_type=F32)


NT = ((1,), (1,))
VM = pl.BlockSpec(memory_space=pltpu.VMEM)
SM = pl.BlockSpec(memory_space=pltpu.SMEM)


def call(kernel, outs, ins, scratch=(), flops=0, nbytes=0, smem=1):
    return pl.pallas_call(
        kernel,
        out_shape=outs,
        in_specs=[SM] * smem + [VM] * (len(ins) - smem),
        out_specs=jax.tree.map(lambda _: VM, outs),
        scratch_shapes=list(scratch),
        compiler_params=pltpu.CompilerParams(vmem_limit_bytes=56 * 2**20),
        cost_estimate=pl.CostEstimate(flops=flops, bytes_accessed=nbytes, transcendentals=0),
    )(*ins)


def norm_rows(values):
    values = values.astype(F32)
    inverse = lax.rsqrt(jnp.mean(values * values, axis=-1, keepdims=True) + EPS)
    return values * inverse, inverse


def normed_kernel(stream, out):
    out[...] = norm_rows(stream[...])[0].astype(BF)


def project_kernel(place, *refs):
    tokens, weights, (out, full) = refs[:4], refs[4:12], refs[12:14]
    column = pl.multiple_of(place[24], 128)
    for group in range(8):
        for shard in range(2):
            row = pl.multiple_of(place[8 + group * 2 + shard], 128)
            for which in range(3):
                full[pl.ds(row, 128), which * 128 : (which + 1) * 128] = weights[group][
                    which, shard * 128 : (shard + 1) * 128, pl.ds(column, 128)
                ]
    for group in range(4):
        for chunk in range(2):
            at = pl.multiple_of(place[group * 2 + chunk], TB)
            out[pl.ds(at, TB), :] = dot(
                tokens[group][chunk * TB : (chunk + 1) * TB, :], full[...]
            ).astype(BF)


def grad_kernel(place, cotan, *refs):
    weights, out = refs[:8], refs[8]
    for group in range(4):
        total = jnp.zeros((TB, 256), F32)
        for side in range(2):
            column = pl.multiple_of(place[side], 1024)
            total = total + dot(cotan[:, pl.ds(column, 1024)], weights[side * 4 + group][...], NT)
        for shard in range(2):
            head = pl.multiple_of(place[2 + group * 2 + shard], 128)
            out[:, pl.ds(head, 128)] = total[:, shard * 128 : (shard + 1) * 128].astype(BF)


def attention_kernel(first, qkv, grad, out, turned, key_t, value_t, key_sum, value_sum):
    key_t[...] = qkv[:, 128:256].T
    value_t[...] = qkv[:, 256:384].T
    key_sum[...] = jnp.zeros_like(key_sum)
    value_sum[...] = jnp.zeros_like(value_sum)
    for block in range(LEN // TB):
        count = (block + 1) * TB
        rows = slice(block * TB, count)
        query = qkv[rows, 0:128]
        grad_rows = grad[rows, :]
        grad_t = grad_rows.T
        scores = dot(qkv[:count, 128:256], query.T)
        key_at = lax.broadcasted_iota(jnp.int32, (count, TB), 0)
        lane = lax.broadcasted_iota(jnp.int32, (1, TB), 1)
        earliest = jnp.where(lane < QBLK, first[0, 2 * block], first[0, 2 * block + 1])
        visible = (key_at >= earliest) & (key_at <= lane + block * TB)
        scores = jnp.where(visible, scores * SCALE, -1e30)
        top = jnp.max(scores, axis=0, keepdims=True)
        raised = jnp.exp(scores - top)
        probs = raised * (1.0 / jnp.sum(raised, axis=0, keepdims=True))
        probs_low = probs.astype(BF)
        attended = dot(value_t[:, :count], probs_low).astype(BF)
        row_dots = jnp.sum(
            grad_t.astype(F32) * attended.astype(F32), axis=0, keepdims=True
        )
        grad_probs = dot(qkv[:count, 256:384], grad_t)
        score_grad = (probs * (grad_probs - row_dots)).astype(BF)
        query_grad = (dot(key_t[:, :count], score_grad) * SCALE).astype(BF)
        key_sum[:count, :] += dot(score_grad, query)
        value_sum[:count, :] += dot(probs_low, grad_rows)
        out[rows, 0:128] = attended.T
        out[rows, 128:256] = query_grad.T
        turned[0:128, rows] = query_grad
        turned[384:512, rows] = attended
    key_grad = (key_sum[...] * SCALE).astype(BF)
    value_grad = value_sum[...].astype(BF)
    out[:, 256:384] = key_grad
    out[:, 384:512] = value_grad
    turned[128:256, :] = key_grad.T
    turned[256:384, :] = value_grad.T


def terms_kernel(place, turned, *refs):
    normed, cotan, out = refs[:4], refs[4:8], refs[8]
    for low, high, tokens in ((0, 384, normed), (384, 512, cotan)):
        total = jnp.zeros((high - low, 512), F32)
        for group in range(4):
            for chunk in range(2):
                at = pl.multiple_of(place[group * 2 + chunk], TB)
                total = total + dot(
                    turned[low:high, pl.ds(at, TB)],
                    tokens[group][chunk * TB : (chunk + 1) * TB, :],
                )
        total = total.astype(BF)
        for part in range(4):
            out[part, low:high, :] = total[:, part * 128 : (part + 1) * 128]


def rebuild_kernel(place, stream, heads, *refs):
    weights, out = refs[:8], refs[8]
    for side in range(2):
        column = pl.multiple_of(place[side], 1024)
        total = jnp.zeros((TB, 1024), F32)
        for group in range(4):
            for shard in range(2):
                head = lax.div(place[2 + group * 2 + shard], 128)
                total = total + dot(
                    heads[head, :, 0:128],
                    weights[side * 4 + group][shard * 128 : (shard + 1) * 128, :],
                )
        here = stream[:, pl.ds(column, 1024)].astype(F32)
        out[:, pl.ds(column, 1024)] = (here - total).astype(BF)


def stream_kernel(place, stream, cotan, heads, *refs):
    weights, out, total = refs[:8], refs[8], refs[9]
    grads = [
        jnp.concatenate(
            [heads[h, :, (which + 1) * 128 : (which + 2) * 128] for h in range(HEADS)], axis=1
        )
        for which in range(3)
    ]
    for group in range(8):
        part = dot(grads[0], weights[group][0], NT)
        part = part + dot(grads[1], weights[group][1], NT)
        part = part + dot(grads[2], weights[group][2], NT)
        for shard in range(2):
            at = pl.multiple_of(place[8 + group * 2 + shard], 128)
            total[:, pl.ds(at, 128)] = part[:, shard * 128 : (shard + 1) * 128]
    normed, inverse = norm_rows(stream[...])
    grad = total[...]
    correction = jnp.mean(grad * normed, axis=-1, keepdims=True)
    out[...] = (cotan[...].astype(F32) + inverse * (grad - normed * correction)).astype(BF)


def shape(dims, kind=BF):
    return jax.ShapeDtypeStruct(dims, kind)


def local(stream_one, stream_two, cotan_one, cotan_two, first_key, w_query, w_key, w_value, w_out):
    dp, seq = lax.axis_index("dp"), lax.axis_index("seq")
    z, x_lo, core = dp // 4, (dp // 2) % 2, dp % 2
    y = seq // 2
    head = 2 * y + core

    token_at, shard_at, heads_at = [], [], []
    for side in range(2):
        for pair in RELATIVE:
            for step in pair:
                where = 2 * ((y + step) % 4) + (core if side == 0 else 1 - core)
                token_at.append(where * TB)
    for side in range(2):
        for far in range(2):
            for pair in RELATIVE:
                for step in pair:
                    where = ((z + step) % 4) * 4 + (x_lo if far == 0 else 1 - x_lo) * 2
                    shard_at.append((where + (core if side == 0 else 1 - core)) * 128)
                    if side == 0:
                        where = ((z + step) % 4) * 2 + (x_lo if far == 0 else 1 - x_lo)
                        heads_at.append(where * 128)
    place = jnp.stack(token_at + shard_at + [head * 128]).astype(jnp.int32)
    place_out = jnp.stack([core * 1024, (1 - core) * 1024] + heads_at).astype(jnp.int32)

    two = send(stream_two[0], SWITCH)
    cot = send(cotan_one[0], SWITCH)
    first = send(first_key, SWITCH)

    normed = call(normed_kernel, shape((TB, D)), [two], smem=0, nbytes=2 * TB * D * 2)
    normed_groups = ring4(normed, Y_UP, Y_DOWN, 0)
    normed_groups = normed_groups + tuple(send(g, CORE) for g in normed_groups)

    is_zero = core == 0
    mine = jnp.where(is_zero, w_out[:, :1024], w_out[:, 1024:])
    theirs = send(jnp.where(is_zero, w_out[:, 1024:], w_out[:, :1024]), CORE)
    head_rows = jnp.where(
        is_zero, jnp.concatenate([mine, theirs], 0), jnp.concatenate([theirs, mine], 0)
    )

    def gather_zx(piece, axis):
        near = ring4(piece, Z_UP, Z_DOWN, axis)
        far = (send(near[0], X_UP), send(near[1], X_DOWN))
        groups = near + far
        return groups + tuple(send(g, CORE) for g in groups)

    out_groups = gather_zx(head_rows, 0)
    in_groups = gather_zx(jnp.stack([w_query, w_key, w_value]), 1)

    cot_groups = ring4(cot, Y_UP, Y_DOWN, 0)
    cot_groups = cot_groups + tuple(send(g, CORE) for g in cot_groups)
    one = send(stream_one[0], SWITCH)
    ctwo = send(cotan_two[0], SWITCH)

    attended_grad = call(
        grad_kernel, shape((TB, 1024)), [place_out, cot, *out_groups], flops=2 * TB * D * 1024,
        nbytes=6 * 2**20,
    )
    by_head = attended_grad.reshape(TB, HEADS, HD).transpose(1, 0, 2)
    grad = lax.all_to_all(
        by_head, AXES, split_axis=0, concat_axis=0, tiled=True, axis_index_groups=GROUP_YC
    ).reshape(LEN, HD)

    qkv = call(
        project_kernel,
        shape((LEN, 384)),
        [place, *normed_groups, *in_groups],
        scratch=[pltpu.VMEM((D, 384), BF)],
        flops=2 * LEN * D * 384,
        nbytes=22 * 2**20,
    )
    by_position, turned = call(
        attention_kernel,
        (shape((LEN, 512)), shape((512, LEN))),
        [first, qkv, grad],
        scratch=[
            pltpu.VMEM((HD, LEN), BF),
            pltpu.VMEM((HD, LEN), BF),
            pltpu.VMEM((LEN, HD), F32),
            pltpu.VMEM((LEN, HD), F32),
        ],
        flops=6 * LEN * LEN * HD,
        nbytes=8 * 2**20,
    )

    wide = pl.BlockSpec((512, 512), lambda i: (0, i))
    terms = pl.pallas_call(
        terms_kernel,
        out_shape=shape((16, 512, 128)),
        grid=(4,),
        in_specs=[SM, pl.BlockSpec((512, LEN), lambda i: (0, 0))] + [wide] * 8,
        out_specs=pl.BlockSpec((4, 512, 128), lambda i: (i, 0, 0)),
        compiler_params=pltpu.CompilerParams(vmem_limit_bytes=56 * 2**20),
        cost_estimate=pl.CostEstimate(
            flops=2 * LEN * D * 512, bytes_accessed=20 * 2**20, transcendentals=0
        ),
    )(place, turned, *normed_groups, *cot_groups)
    spread = lax.all_to_all(
        terms, AXES, split_axis=0, concat_axis=0, tiled=True, axis_index_groups=GROUP_ZX
    )
    summed = jnp.sum(spread.astype(F32), axis=0).astype(BF)

    heads = lax.all_to_all(
        by_position.reshape(8, TB, 512),
        AXES,
        split_axis=0,
        concat_axis=0,
        tiled=True,
        axis_index_groups=GROUP_YC,
    )

    summed = send(summed, SWITCH)
    other = send(summed, HALF)
    x_hi = seq % 2
    pair = jnp.where(x_hi == 0, jnp.stack([summed, other]), jnp.stack([other, summed]))
    low, high = ring4(pair, Y_UP, Y_DOWN, 1)
    ring = jnp.stack([low[:, :512], high[:, :512], high[:, 512:], low[:, 512:]])
    ring = jnp.roll(ring, y, axis=0).reshape(HEADS, 4, HD, 128)

    def rows_of(which):
        return ring[:, which].transpose(2, 0, 1).reshape(128, 1024).astype(F32)

    out_rows = lax.all_to_all(
        ring[:, 3].reshape(16, 64, 128), "dp", split_axis=0, concat_axis=0, tiled=True
    )
    grad_out = out_rows.transpose(1, 0, 2).reshape(64, D).astype(F32)

    input_one = call(
        rebuild_kernel,
        shape((TB, D)),
        [place_out, one, heads, *out_groups],
        flops=2 * TB * D * 1024,
        nbytes=8 * 2**20,
    )
    grad_two = call(
        stream_kernel,
        shape((TB, D)),
        [place, two, ctwo, heads, *in_groups],
        scratch=[pltpu.VMEM((TB, D), F32)],
        flops=6 * TB * D * 1024,
        nbytes=17 * 2**20,
    )
    input_one = send(input_one, SWITCH)[None]
    grad_two = send(grad_two, SWITCH)[None]
    return (input_one, grad_two, rows_of(0), rows_of(1), rows_of(2), grad_out)


def solution(mesh):
    tokens, rows = P("dp", "seq", None), P("dp", None)
    return jax.shard_map(
        local,
        mesh=mesh,
        in_specs=(tokens,) * 4 + (rows,) * 5,
        out_specs=(tokens, tokens, rows, rows, rows, rows),
        check_vma=False,
    )
```

```python
import jax
import jax.numpy as jnp
from jax import lax
from jax.experimental import pallas as pl
from jax.experimental.pallas import tpu as pltpu
from jax.sharding import PartitionSpec as P

HEADS = 8
HD = 128
QBLK = 128
EPS = 1e-06
SCALE = HD ** (-0.5)
AXES = ("dp", "seq")
BF = jnp.bfloat16
F32 = jnp.float32
TB = 256
LEN = 2048
D = 2048

COORDS = [
    (z, xl, c, y, xh)
    for z in range(4)
    for xl in range(2)
    for c in range(2)
    for y in range(4)
    for xh in range(2)
]


def flat(z, xl, c, y, xh):
    return (z * 4 + xl * 2 + c) * 8 + y * 2 + xh


def perm(move):
    return [(flat(*at), flat(*move(*at))) for at in COORDS]


SWITCH = perm(lambda z, xl, c, y, xh: (z, 1 - xl, xh, y, c))
CROSS = perm(lambda z, xl, c, y, xh: (z, 1 - xl, xh, y, 1 - c))
CORE = perm(lambda z, xl, c, y, xh: (z, xl, 1 - c, y, xh))
Y_UP = perm(lambda z, xl, c, y, xh: (z, xl, c, (y + 1) % 4, xh))
Y_FAR = perm(lambda z, xl, c, y, xh: (z, xl, c, (y + 2) % 4, xh))
Y_DOWN = perm(lambda z, xl, c, y, xh: (z, xl, c, (y - 1) % 4, xh))
GROUP_YC = [
    [flat(z, xl, c, y, xh) for y in range(4) for c in range(2)]
    for z in range(4)
    for xl in range(2)
    for xh in range(2)
]
GROUP_ZX = [
    [flat(z, 1 - xl, c, y, xh) for z in range(4) for xl in range(2) for xh in range(2)]
    for y in range(4)
    for c in range(2)
]


def send(value, pairs):
    return lax.ppermute(value, AXES, pairs)


def ring_first(piece, up, down):
    return send(piece, up), send(piece, down)


def ring_second(piece, below, above, up, down):
    half = piece.shape[0] // 2
    far_low, far_high = send(below[:half], up), send(above[half:], down)
    return (
        jnp.concatenate([piece, below], axis=0),
        jnp.concatenate([above, far_low, far_high], axis=0),
    )


def after(values, *earlier):
    return lax.optimization_barrier((tuple(values), earlier))[0]


RELATIVE = ((0, -1), (1, 2))


def dot(a, b, dims=((1,), (0,))):
    return lax.dot_general(a, b, (dims, ((), ())), preferred_element_type=F32)


NT = ((1,), (1,))
VM = pl.BlockSpec(memory_space=pltpu.VMEM)
SM = pl.BlockSpec(memory_space=pltpu.SMEM)


def call(kernel, outs, ins, scratch=(), flops=0, nbytes=0, smem=1):
    return pl.pallas_call(
        kernel,
        out_shape=outs,
        in_specs=[SM] * smem + [VM] * (len(ins) - smem),
        out_specs=jax.tree.map(lambda _: VM, outs),
        scratch_shapes=list(scratch),
        compiler_params=pltpu.CompilerParams(vmem_limit_bytes=28 * 2**20),
        cost_estimate=pl.CostEstimate(flops=flops, bytes_accessed=nbytes, transcendentals=0),
    )(*ins)


def norm_rows(values):
    values = values.astype(F32)
    inverse = lax.rsqrt(jnp.mean(values * values, axis=-1, keepdims=True) + EPS)
    return values * inverse, inverse


def normed_kernel(stream, out):
    out[...] = norm_rows(stream[...])[0].astype(BF)


def out_kernel(gathered, cotan, full, grad):
    for h in range(HEADS):
        for part in range(2):
            at = (2 * h + part) * 128
            rows = slice(h * HD + part * 64, h * HD + part * 64 + 64)
            full[rows, 0:1024] = gathered[at : at + 64, :]
            full[rows, 1024:D] = gathered[at + 64 : at + 128, :]
    for h in range(0, HEADS, 2):
        product = dot(cotan[...], full[h * HD : (h + 2) * HD, :], NT).astype(BF)
        grad[h] = product[:, :HD]
        grad[h + 1] = product[:, HD:]


def project_kernel(place, part0, part1, part2, part3, query, key, value, out, held, weight, sems):
    parts = (part0, part1, part2, part3)
    copies = [
        pltpu.make_async_copy(part, held.at[group], sems.at[group])
        for group, part in enumerate(parts)
    ]
    for copy in copies:
        copy.start()
    column = pl.multiple_of(place[8], 128)
    for which, source in enumerate((query, key, value)):
        weight[:, which * HD : (which + 1) * HD] = source[:, pl.ds(column, HD)]
    for group in range(4):
        copies[group].wait()
        for chunk in range(2):
            at = pl.multiple_of(place[group * 2 + chunk], TB)
            out[pl.ds(at, TB), :] = dot(
                held[group, chunk * TB : (chunk + 1) * TB, :], weight[...]
            ).astype(BF)


def attention_kernel(first, qkv, grad, out, turned, key_t, value_t, key_sum, value_sum):
    key_t[...] = qkv[:, 128:256].T
    value_t[...] = qkv[:, 256:384].T
    key_sum[...] = jnp.zeros_like(key_sum)
    value_sum[...] = jnp.zeros_like(value_sum)
    for block in range(LEN // TB):
        count = (block + 1) * TB
        rows = slice(block * TB, count)
        query = qkv[rows, 0:128]
        grad_rows = grad[rows, :]
        grad_t = grad_rows.T
        scores = dot(qkv[:count, 128:256], query.T)
        key_at = lax.broadcasted_iota(jnp.int32, (count, TB), 0)
        lane = lax.broadcasted_iota(jnp.int32, (1, TB), 1)
        earliest = jnp.where(lane < QBLK, first[0, 2 * block], first[0, 2 * block + 1])
        visible = (key_at >= earliest) & (key_at <= lane + block * TB)
        scores = jnp.where(visible, scores * SCALE, -1e30)
        top = jnp.max(scores, axis=0, keepdims=True)
        raised = jnp.exp(scores - top)
        probs = raised * (1.0 / jnp.sum(raised, axis=0, keepdims=True))
        probs_low = probs.astype(BF)
        attended = dot(value_t[:, :count], probs_low).astype(BF)
        row_dots = jnp.sum(
            grad_t.astype(F32) * attended.astype(F32), axis=0, keepdims=True
        )
        grad_probs = dot(qkv[:count, 256:384], grad_t)
        score_grad = (probs * (grad_probs - row_dots)).astype(BF)
        query_grad = (dot(key_t[:, :count], score_grad) * SCALE).astype(BF)
        key_sum[:count, :] += dot(score_grad, query)
        value_sum[:count, :] += dot(probs_low, grad_rows)
        out[rows, 0:128] = attended.T
        out[rows, 128:256] = query_grad.T
        turned[0:128, rows] = query_grad
        turned[384:512, rows] = attended
    key_grad = (key_sum[...] * SCALE).astype(BF)
    value_grad = value_sum[...].astype(BF)
    out[:, 256:384] = key_grad
    out[:, 384:512] = value_grad
    turned[128:256, :] = key_grad.T
    turned[256:384, :] = value_grad.T


def terms_kernel(place, turned, *refs):
    normed, cotan, out, ordered = refs[:4], refs[4:8], refs[8], refs[9]

    @pl.when(pl.program_id(0) == 0)
    def _():
        for slot in range(8):
            at = pl.multiple_of(place[slot], TB)
            ordered[:, slot * TB : (slot + 1) * TB] = turned[:, pl.ds(at, TB)]

    for low, high, tokens in ((0, 384, normed), (384, 512, cotan)):
        total = jnp.zeros((high - low, 512), F32)
        size = LEN // len(tokens)
        for group, piece in enumerate(tokens):
            total = total + dot(
                ordered[low:high, group * size : (group + 1) * size], piece[...]
            )
        total = total.astype(BF)
        for part in range(4):
            out[part, low:high, :] = total[:, part * 128 : (part + 1) * 128]


def stream_kernel(
    place, stream, heads0, heads1, heads2, heads3, w_in, w_out, out_one, out_two, total, grads
):
    step = pl.program_id(0)

    @pl.when(step == 0)
    def _():
        for group, heads in enumerate((heads0, heads1, heads2, heads3)):
            for side in range(2):
                at = pl.multiple_of(place[9 + group * 2 + side], HD)
                for which in range(4):
                    grads[which, :, pl.ds(at, HD)] = heads[side, :, which * HD : (which + 1) * HD]

    part = dot(grads[1], w_in[:, 0:1024], NT)
    part = part + dot(grads[2], w_in[:, 1024:2048], NT)
    part = part + dot(grads[3], w_in[:, 2048:3072], NT)
    columns = pl.ds(pl.multiple_of(step * 512, 512), 512)
    total[:, columns] = part
    out_one[:, columns] = dot(grads[0], w_out[...]).astype(BF)

    @pl.when(step == 3)
    def _():
        normed, inverse = norm_rows(stream[...])
        grad = total[...]
        correction = jnp.mean(grad * normed, axis=-1, keepdims=True)
        out_two[...] = (inverse * (grad - normed * correction)).astype(BF)


def shape(dims, kind=BF):
    return jax.ShapeDtypeStruct(dims, kind)


def local(stream_one, stream_two, cotan_one, cotan_two, first_key, w_query, w_key, w_value, w_out):
    dp, seq = lax.axis_index("dp"), lax.axis_index("seq")
    core, y = dp % 2, seq // 2

    token_at = []
    for side in range(2):
        for pair in RELATIVE:
            for step in pair:
                where = 2 * ((y + step) % 4) + (core if side == 0 else 1 - core)
                token_at.append(where * TB)
    head_at = [
        (2 * ((y + step) % 4) + (core if side == 0 else 1 - core)) * HD
        for step in (0, -1, 1, 2)
        for side in range(2)
    ]
    place = jnp.stack(token_at + [core * HD] + head_at).astype(jnp.int32)

    two = send(stream_two[0], SWITCH)
    first = send(first_key, SWITCH)
    (cot,) = after([cotan_one[0]], two)
    cot = send(cot, SWITCH)

    normed = call(normed_kernel, shape((TB, D)), [two], smem=0, nbytes=2 * TB * D * 2)
    below, above = ring_first(normed, Y_UP, Y_DOWN)
    normed_groups = after(ring_second(normed, below, above, Y_UP, Y_DOWN), cot)
    (cot_first,) = after([cot], normed_groups[1])
    normed_groups = normed_groups + tuple(send(g, CORE) for g in normed_groups)

    slim = jnp.concatenate(
        [jnp.concatenate([w_out[:, :1024], w_out[:, 1024:]], axis=0)]
        + [lax.dynamic_slice_in_dim(w, y * 256, 256, axis=1) for w in (w_query, w_key, w_value)],
        axis=1,
    )
    slim = lax.all_gather(slim, "dp", axis=0, tiled=True)
    w_query, w_key, w_value, _ = lax.optimization_barrier((w_query, w_key, w_value, normed))
    full_in = lax.all_gather(
        jnp.concatenate([w_query, w_key, w_value], axis=1), "dp", axis=0, tiled=True
    )

    full_out, by_head = pl.pallas_call(
        out_kernel,
        out_shape=(shape((1024, D)), shape((HEADS, TB, HD))),
        grid=(1,),
        in_specs=[
            pl.BlockSpec((D, 1024), lambda i: (0, 0)),
            pl.BlockSpec((TB, D), lambda i: (0, 0)),
        ],
        out_specs=(
            pl.BlockSpec((1024, D), lambda i: (0, 0)),
            pl.BlockSpec((HEADS, TB, HD), lambda i: (0, 0, 0)),
        ),
        compiler_params=pltpu.CompilerParams(vmem_limit_bytes=30 * 2**20),
        cost_estimate=pl.CostEstimate(
            flops=6 * 10**9, bytes_accessed=9 * 2**20, transcendentals=0
        ),
    )(slim, cot)
    grad = lax.all_to_all(
        by_head, AXES, split_axis=0, concat_axis=0, tiled=True, axis_index_groups=GROUP_YC
    ).reshape(LEN, HD)

    cot_below, cot_above = ring_first(cot_first, Y_UP, Y_DOWN)
    cot_below, cot_above = after([cot_below, cot_above], grad)
    normed_groups = after(normed_groups, grad)
    cot_groups = ring_second(cot, cot_below, cot_above, Y_UP, Y_DOWN)
    columns = [pl.BlockSpec((D, 256), lambda i, which=which: (0, 4 + which)) for which in range(3)]
    qkv = pl.pallas_call(
        project_kernel,
        out_shape=shape((LEN, 384)),
        grid=(1,),
        in_specs=[SM] + [pl.BlockSpec(memory_space=pl.ANY)] * 4 + columns,
        out_specs=pl.BlockSpec((LEN, 384), lambda i: (0, 0)),
        scratch_shapes=[
            pltpu.VMEM((4, 512, D), BF),
            pltpu.VMEM((D, 384), BF),
            pltpu.SemaphoreType.DMA((4,)),
        ],
        compiler_params=pltpu.CompilerParams(vmem_limit_bytes=30 * 2**20),
        cost_estimate=pl.CostEstimate(
            flops=9 * 10**9, bytes_accessed=13 * 2**20, transcendentals=0
        ),
    )(place, *normed_groups, slim, slim, slim)
    (qkv,) = after([qkv], *cot_groups)
    by_position, turned = call(
        attention_kernel,
        (shape((LEN, 512)), shape((512, LEN))),
        [first, qkv, grad],
        scratch=[
            pltpu.VMEM((HD, LEN), BF),
            pltpu.VMEM((HD, LEN), BF),
            pltpu.VMEM((LEN, HD), F32),
            pltpu.VMEM((LEN, HD), F32),
        ],
        flops=20 * 10**9,
        nbytes=8 * 2**20,
    )

    blocks = by_position.reshape(4, 2, TB, 512)
    mine = lax.dynamic_index_in_dim(blocks, core, axis=1, keepdims=False)
    theirs = send(lax.dynamic_index_in_dim(blocks, 1 - core, axis=1, keepdims=False), CORE)
    def block_for(step):
        return jnp.stack(
            [
                lax.dynamic_index_in_dim(values, (y + step) % 4, axis=0, keepdims=False)
                for values in (mine, theirs)
            ]
        )

    heads = [
        block_for(0),
        send(block_for(1), Y_UP),
        send(block_for(-1), Y_DOWN),
        send(block_for(2), Y_FAR),
    ]
    cot_groups = after(cot_groups, theirs)
    cot_groups = cot_groups + tuple(send(g, CORE) for g in cot_groups)

    wide = pl.BlockSpec((512, 512), lambda i: (0, i))
    terms = pl.pallas_call(
        terms_kernel,
        out_shape=shape((16, 512, 128)),
        grid=(4,),
        in_specs=[SM, pl.BlockSpec((512, LEN), lambda i: (0, 0))] + [wide] * 8,
        out_specs=pl.BlockSpec((4, 512, 128), lambda i: (i, 0, 0)),
        scratch_shapes=[pltpu.VMEM((512, LEN), BF)],
        compiler_params=pltpu.CompilerParams(vmem_limit_bytes=26 * 2**20),
        cost_estimate=pl.CostEstimate(
            flops=12 * 10**9, bytes_accessed=20 * 2**20, transcendentals=0
        ),
    )(place, turned, *normed_groups, *cot_groups)
    (terms,) = after([terms], *heads)
    spread = lax.all_to_all(
        terms, AXES, split_axis=0, concat_axis=0, tiled=True, axis_index_groups=GROUP_ZX
    )
    rows_spec = pl.BlockSpec((TB, D), lambda i: (0, 0))
    mixed, change = pl.pallas_call(
        stream_kernel,
        out_shape=(shape((TB, D)), shape((TB, D))),
        grid=(4,),
        in_specs=[SM]
        + [rows_spec]
        + [pl.BlockSpec((2, TB, 512), lambda i: (0, 0, 0))] * 4
        + [pl.BlockSpec((512, 3072), lambda i: (i, 0))]
        + [pl.BlockSpec((1024, 512), lambda i: (0, i))],
        out_specs=(rows_spec, rows_spec),
        scratch_shapes=[pltpu.VMEM((TB, D), F32), pltpu.VMEM((4, TB, 1024), BF)],
        compiler_params=pltpu.CompilerParams(vmem_limit_bytes=30 * 2**20),
        cost_estimate=pl.CostEstimate(
            flops=14 * 10**9, bytes_accessed=22 * 2**20, transcendentals=0
        ),
    )(place, two, *heads, full_in, full_out)
    (spread,) = after([spread], mixed, change)
    summed = jnp.sum(spread.astype(F32), axis=0).astype(BF)
    near, cross = send(summed, SWITCH), send(summed, CROSS)
    x_zero = seq % 2 == 0
    pair = jnp.where(x_zero, jnp.stack([near, cross]), jnp.stack([cross, near]))

    def all_heads(piece):
        below, above, far = send(piece, Y_UP), send(piece, Y_DOWN), send(piece, Y_FAR)
        return jnp.roll(jnp.stack([piece, above, far, below]), y, axis=0)

    out_rows = lax.all_to_all(
        all_heads(pair[:, 384:]).reshape(16, 64, 128),
        "dp",
        split_axis=0,
        concat_axis=0,
        tiled=True,
    )
    grad_out = out_rows.transpose(1, 0, 2).reshape(64, D).astype(F32)
    in_rows = all_heads(pair[:, :384]).reshape(HEADS, 3, HD, 128)

    def rows_of(which):
        return in_rows[:, which].transpose(2, 0, 1).reshape(128, 1024).astype(F32)

    mixed, change = after([mixed, change], near, cross)
    mixed, change = send(mixed, SWITCH), send(change, SWITCH)
    input_one = (stream_one.astype(F32) - mixed[None].astype(F32)).astype(BF)
    grad_two = (cotan_two.astype(F32) + change[None].astype(F32)).astype(BF)
    return (input_one, grad_two, rows_of(0), rows_of(1), rows_of(2), grad_out)


def solution(mesh):
    tokens, rows = P("dp", "seq", None), P("dp", None)
    return jax.shard_map(
        local,
        mesh=mesh,
        in_specs=(tokens,) * 4 + (rows,) * 5,
        out_specs=(tokens, tokens, rows, rows, rows, rows),
        check_vma=False,
    )
```

```python
import jax
import jax.numpy as jnp
from jax import lax
from jax.experimental import pallas as pl
from jax.experimental.pallas import tpu as pltpu
from jax.sharding import PartitionSpec as P

HEADS = 8
HD = 128
QBLK = 128
EPS = 1e-06
SCALE = HD ** (-0.5)
AXES = ("dp", "seq")
BF = jnp.bfloat16
F32 = jnp.float32
TB = 256
LEN = 2048
D = 2048

COORDS = [
    (z, xl, c, y, xh)
    for z in range(4)
    for xl in range(2)
    for c in range(2)
    for y in range(4)
    for xh in range(2)
]


def flat(z, xl, c, y, xh):
    return (z * 4 + xl * 2 + c) * 8 + y * 2 + xh


def perm(move):
    return [(flat(*at), flat(*move(*at))) for at in COORDS]


SWITCH = perm(lambda z, xl, c, y, xh: (z, 1 - xl, xh, y, c))
CROSS = perm(lambda z, xl, c, y, xh: (z, 1 - xl, xh, y, 1 - c))
CORE = perm(lambda z, xl, c, y, xh: (z, xl, 1 - c, y, xh))
Y_UP = perm(lambda z, xl, c, y, xh: (z, xl, c, (y + 1) % 4, xh))
Y_FAR = perm(lambda z, xl, c, y, xh: (z, xl, c, (y + 2) % 4, xh))
Y_DOWN = perm(lambda z, xl, c, y, xh: (z, xl, c, (y - 1) % 4, xh))
GROUP_YC = [
    [flat(z, xl, c, y, xh) for y in range(4) for c in range(2)]
    for z in range(4)
    for xl in range(2)
    for xh in range(2)
]
GROUP_ZX = [
    [flat(z, 1 - xl, c, y, xh) for z in range(4) for xl in range(2) for xh in range(2)]
    for y in range(4)
    for c in range(2)
]


def send(value, pairs):
    return lax.ppermute(value, AXES, pairs)


def ring_first(piece, up, down):
    return send(piece, up), send(piece, down)


def ring_second(below, above, up, down):
    half = below.shape[0] // 2
    return send(below[:half], up), send(above[half:], down)


def after(values, *earlier):
    return lax.optimization_barrier((tuple(values), earlier))[0]


STEPS = (0, -1, 1, 2)
SIZES = (TB, TB, TB, TB // 2, TB // 2) * 2


def dot(a, b, dims=((1,), (0,))):
    return lax.dot_general(a, b, (dims, ((), ())), preferred_element_type=F32)


NT = ((1,), (1,))
VM = pl.BlockSpec(memory_space=pltpu.VMEM)
SM = pl.BlockSpec(memory_space=pltpu.SMEM)


def call(kernel, outs, ins, scratch=(), flops=0, nbytes=0, smem=1):
    return pl.pallas_call(
        kernel,
        out_shape=outs,
        in_specs=[SM] * smem + [VM] * (len(ins) - smem),
        out_specs=jax.tree.map(lambda _: VM, outs),
        scratch_shapes=list(scratch),
        compiler_params=pltpu.CompilerParams(vmem_limit_bytes=28 * 2**20),
        cost_estimate=pl.CostEstimate(flops=flops, bytes_accessed=nbytes, transcendentals=0),
    )(*ins)


def norm_rows(values):
    values = values.astype(F32)
    inverse = lax.rsqrt(jnp.mean(values * values, axis=-1, keepdims=True) + EPS)
    return values * inverse, inverse


def normed_kernel(stream, out):
    out[...] = norm_rows(stream[...])[0].astype(BF)


def out_kernel(gathered, cotan, full, grad):
    for h in range(HEADS):
        for part in range(2):
            at = (2 * h + part) * 128
            rows = slice(h * HD + part * 64, h * HD + part * 64 + 64)
            full[rows, 0:1024] = gathered[at : at + 64, :]
            full[rows, 1024:D] = gathered[at + 64 : at + 128, :]
    for h in range(0, HEADS, 2):
        product = dot(cotan[...], full[h * HD : (h + 2) * HD, :], NT).astype(BF)
        grad[h] = product[:, :HD]
        grad[h + 1] = product[:, HD:]


def project_kernel(place, *refs):
    parts, (query, key, value, out, held, weight, sems) = refs[:10], refs[10:]
    copies, at = [], 0
    for slot, (part, size) in enumerate(zip(parts, SIZES)):
        copies.append(
            pltpu.make_async_copy(part, held.at[pl.ds(at, size), :], sems.at[slot])
        )
        at += size
    for copy in copies:
        copy.start()
    column = pl.multiple_of(place[8], 128)
    for which, source in enumerate((query, key, value)):
        weight[:, which * HD : (which + 1) * HD] = source[:, pl.ds(column, HD)]
    for side in range(2):
        for step in range(4):
            copies[side * 5 + step].wait()
            if step == 3:
                copies[side * 5 + 4].wait()
            slot = side * 4 + step
            at = pl.multiple_of(place[slot], TB)
            out[pl.ds(at, TB), :] = dot(
                held[slot * TB : (slot + 1) * TB, :], weight[...]
            ).astype(BF)


def attention_kernel(first, qkv, grad, out, turned, key_t, value_t, key_sum, value_sum):
    key_t[...] = qkv[:, 128:256].T
    value_t[...] = qkv[:, 256:384].T
    key_sum[...] = jnp.zeros_like(key_sum)
    value_sum[...] = jnp.zeros_like(value_sum)
    for block in range(LEN // TB):
        count = (block + 1) * TB
        rows = slice(block * TB, count)
        query = qkv[rows, 0:128]
        grad_rows = grad[rows, :]
        grad_t = grad_rows.T
        scores = dot(qkv[:count, 128:256], query.T)
        key_at = lax.broadcasted_iota(jnp.int32, (count, TB), 0)
        lane = lax.broadcasted_iota(jnp.int32, (1, TB), 1)
        earliest = jnp.where(lane < QBLK, first[0, 2 * block], first[0, 2 * block + 1])
        visible = (key_at >= earliest) & (key_at <= lane + block * TB)
        scores = jnp.where(visible, scores * SCALE, -1e30)
        top = jnp.max(scores, axis=0, keepdims=True)
        raised = jnp.exp(scores - top)
        probs = raised * (1.0 / jnp.sum(raised, axis=0, keepdims=True))
        probs_low = probs.astype(BF)
        attended = dot(value_t[:, :count], probs_low).astype(BF)
        row_dots = jnp.sum(
            grad_t.astype(F32) * attended.astype(F32), axis=0, keepdims=True
        )
        grad_probs = dot(qkv[:count, 256:384], grad_t)
        score_grad = (probs * (grad_probs - row_dots)).astype(BF)
        query_grad = (dot(key_t[:, :count], score_grad) * SCALE).astype(BF)
        key_sum[:count, :] += dot(score_grad, query)
        value_sum[:count, :] += dot(probs_low, grad_rows)
        out[rows, 0:128] = attended.T
        out[rows, 128:256] = query_grad.T
        turned[0:128, rows] = query_grad
        turned[384:512, rows] = attended
    key_grad = (key_sum[...] * SCALE).astype(BF)
    value_grad = value_sum[...].astype(BF)
    out[:, 256:384] = key_grad
    out[:, 384:512] = value_grad
    turned[128:256, :] = key_grad.T
    turned[256:384, :] = value_grad.T


def terms_kernel(place, turned, *refs):
    normed, cotan, out, ordered = refs[:10], refs[10:20], refs[20], refs[21]

    @pl.when(pl.program_id(0) == 0)
    def _():
        for slot in range(8):
            at = pl.multiple_of(place[slot], TB)
            ordered[:, slot * TB : (slot + 1) * TB] = turned[:, pl.ds(at, TB)]

    for low, high, tokens in ((0, 384, normed), (384, 512, cotan)):
        rows = jnp.concatenate([piece[...] for piece in tokens], axis=0)
        total = dot(ordered[low:high, :], rows)
        total = total.astype(BF)
        for part in range(4):
            out[part, low:high, :] = total[:, part * 128 : (part + 1) * 128]


def stream_kernel(
    place, stream, heads0, heads1, heads2, heads3, w_in, w_out, out_one, out_two, total, grads
):
    step = pl.program_id(0)

    @pl.when(step == 0)
    def _():
        for group, heads in enumerate((heads0, heads1, heads2, heads3)):
            for side in range(2):
                at = pl.multiple_of(place[9 + group * 2 + side], HD)
                for which in range(4):
                    grads[which, :, pl.ds(at, HD)] = heads[side, :, which * HD : (which + 1) * HD]

    part = dot(grads[1], w_in[:, 0:1024], NT)
    part = part + dot(grads[2], w_in[:, 1024:2048], NT)
    part = part + dot(grads[3], w_in[:, 2048:3072], NT)
    columns = pl.ds(pl.multiple_of(step * 512, 512), 512)
    total[:, columns] = part
    out_one[:, columns] = dot(grads[0], w_out[...]).astype(BF)

    @pl.when(step == 3)
    def _():
        normed, inverse = norm_rows(stream[...])
        grad = total[...]
        correction = jnp.mean(grad * normed, axis=-1, keepdims=True)
        out_two[...] = (inverse * (grad - normed * correction)).astype(BF)


def shape(dims, kind=BF):
    return jax.ShapeDtypeStruct(dims, kind)


def local(stream_one, stream_two, cotan_one, cotan_two, first_key, w_query, w_key, w_value, w_out):
    dp, seq = lax.axis_index("dp"), lax.axis_index("seq")
    core, y = dp % 2, seq // 2

    token_at = []
    for side in range(2):
        for step in STEPS:
            where = 2 * ((y + step) % 4) + (core if side == 0 else 1 - core)
            token_at.append(where * TB)
    head_at = [
        (2 * ((y + step) % 4) + (core if side == 0 else 1 - core)) * HD
        for step in STEPS
        for side in range(2)
    ]
    place = jnp.stack(token_at + [core * HD] + head_at).astype(jnp.int32)

    two = send(stream_two[0], SWITCH)
    first = send(first_key, SWITCH)
    (cot,) = after([cotan_one[0]], two)
    cot = send(cot, SWITCH)

    normed = call(normed_kernel, shape((TB, D)), [two], smem=0, nbytes=2 * TB * D * 2)
    below, above = ring_first(normed, Y_UP, Y_DOWN)
    far = after(ring_second(below, above, Y_UP, Y_DOWN), cot)
    normed_pieces = [normed, below, above, *far]
    normed_pieces = normed_pieces + [send(piece, CORE) for piece in normed_pieces]

    slim = jnp.concatenate(
        [jnp.concatenate([w_out[:, :1024], w_out[:, 1024:]], axis=0)]
        + [lax.dynamic_slice_in_dim(w, y * 256, 256, axis=1) for w in (w_query, w_key, w_value)],
        axis=1,
    )
    slim = lax.all_gather(slim, "dp", axis=0, tiled=True)
    w_query, w_key, w_value, _ = lax.optimization_barrier((w_query, w_key, w_value, normed))
    full_in = lax.all_gather(
        jnp.concatenate([w_query, w_key, w_value], axis=1), "dp", axis=0, tiled=True
    )

    full_out, by_head = pl.pallas_call(
        out_kernel,
        out_shape=(shape((1024, D)), shape((HEADS, TB, HD))),
        grid=(1,),
        in_specs=[
            pl.BlockSpec((D, 1024), lambda i: (0, 0)),
            pl.BlockSpec((TB, D), lambda i: (0, 0)),
        ],
        out_specs=(
            pl.BlockSpec((1024, D), lambda i: (0, 0)),
            pl.BlockSpec((HEADS, TB, HD), lambda i: (0, 0, 0)),
        ),
        compiler_params=pltpu.CompilerParams(vmem_limit_bytes=30 * 2**20),
        cost_estimate=pl.CostEstimate(
            flops=6 * 10**9, bytes_accessed=9 * 2**20, transcendentals=0
        ),
    )(slim, cot)
    grad = lax.all_to_all(
        by_head, AXES, split_axis=0, concat_axis=0, tiled=True, axis_index_groups=GROUP_YC
    ).reshape(LEN, HD)

    (cot_first,) = after([cot], far[1], slim)
    cot_below, cot_above = ring_first(cot_first, Y_UP, Y_DOWN)
    cot_below, cot_above = after([cot_below, cot_above], grad)
    cot_far = ring_second(cot_below, cot_above, Y_UP, Y_DOWN)
    columns = [pl.BlockSpec((D, 256), lambda i, which=which: (0, 4 + which)) for which in range(3)]
    qkv = pl.pallas_call(
        project_kernel,
        out_shape=shape((LEN, 384)),
        grid=(1,),
        in_specs=[SM] + [pl.BlockSpec(memory_space=pl.ANY)] * 10 + columns,
        out_specs=pl.BlockSpec((LEN, 384), lambda i: (0, 0)),
        scratch_shapes=[
            pltpu.VMEM((LEN, D), BF),
            pltpu.VMEM((D, 384), BF),
            pltpu.SemaphoreType.DMA((10,)),
        ],
        compiler_params=pltpu.CompilerParams(vmem_limit_bytes=30 * 2**20),
        cost_estimate=pl.CostEstimate(
            flops=9 * 10**9, bytes_accessed=13 * 2**20, transcendentals=0
        ),
    )(place, *normed_pieces, slim, slim, slim)
    cot_near = [cot, cot_below, cot_above]
    cot_swapped = [send(piece, CORE) for piece in cot_near]
    (qkv,) = after([qkv], *cot_far, *cot_swapped)
    by_position, turned = call(
        attention_kernel,
        (shape((LEN, 512)), shape((512, LEN))),
        [first, qkv, grad],
        scratch=[
            pltpu.VMEM((HD, LEN), BF),
            pltpu.VMEM((HD, LEN), BF),
            pltpu.VMEM((LEN, HD), F32),
            pltpu.VMEM((LEN, HD), F32),
        ],
        flops=20 * 10**9,
        nbytes=8 * 2**20,
    )

    blocks = by_position.reshape(4, 2, TB, 512)
    mine = lax.dynamic_index_in_dim(blocks, core, axis=1, keepdims=False)
    theirs = send(lax.dynamic_index_in_dim(blocks, 1 - core, axis=1, keepdims=False), CORE)
    def block_for(step):
        return jnp.stack(
            [
                lax.dynamic_index_in_dim(values, (y + step) % 4, axis=0, keepdims=False)
                for values in (mine, theirs)
            ]
        )

    heads = [
        block_for(0),
        send(block_for(1), Y_UP),
        send(block_for(-1), Y_DOWN),
        send(block_for(2), Y_FAR),
    ]
    cot_last = [send(piece, CORE) for piece in after(cot_far, turned)]
    cot_pieces = [*cot_near, *cot_far, *cot_swapped, *cot_last]

    wide = [pl.BlockSpec((size, 512), lambda i: (0, i)) for size in SIZES]
    terms = pl.pallas_call(
        terms_kernel,
        out_shape=shape((16, 512, 128)),
        grid=(4,),
        in_specs=[SM, pl.BlockSpec((512, LEN), lambda i: (0, 0))] + wide * 2,
        out_specs=pl.BlockSpec((4, 512, 128), lambda i: (i, 0, 0)),
        scratch_shapes=[pltpu.VMEM((512, LEN), BF)],
        compiler_params=pltpu.CompilerParams(vmem_limit_bytes=26 * 2**20),
        cost_estimate=pl.CostEstimate(
            flops=12 * 10**9, bytes_accessed=20 * 2**20, transcendentals=0
        ),
    )(place, turned, *normed_pieces, *cot_pieces)
    (terms,) = after([terms], heads[3])
    spread = lax.all_to_all(
        terms, AXES, split_axis=0, concat_axis=0, tiled=True, axis_index_groups=GROUP_ZX
    )
    rows_spec = pl.BlockSpec((TB, D), lambda i: (0, 0))
    mixed, change = pl.pallas_call(
        stream_kernel,
        out_shape=(shape((TB, D)), shape((TB, D))),
        grid=(4,),
        in_specs=[SM]
        + [rows_spec]
        + [pl.BlockSpec((2, TB, 512), lambda i: (0, 0, 0))] * 4
        + [pl.BlockSpec((512, 3072), lambda i: (i, 0))]
        + [pl.BlockSpec((1024, 512), lambda i: (0, i))],
        out_specs=(rows_spec, rows_spec),
        scratch_shapes=[pltpu.VMEM((TB, D), F32), pltpu.VMEM((4, TB, 1024), BF)],
        compiler_params=pltpu.CompilerParams(vmem_limit_bytes=30 * 2**20),
        cost_estimate=pl.CostEstimate(
            flops=14 * 10**9, bytes_accessed=22 * 2**20, transcendentals=0
        ),
    )(place, two, *heads, full_in, full_out)
    (spread,) = after([spread], mixed, change)
    summed = jnp.sum(spread.astype(F32), axis=0).astype(BF)
    near, cross = send(summed, SWITCH), send(summed, CROSS)
    mixed = send(mixed, SWITCH)
    near, cross = after([near, cross], mixed)
    (change,) = after([change], near, cross)
    change = send(change, SWITCH)
    x_zero = seq % 2 == 0
    pair = jnp.where(x_zero, jnp.stack([near, cross]), jnp.stack([cross, near]))

    def all_heads(piece):
        below, above, far = send(piece, Y_UP), send(piece, Y_DOWN), send(piece, Y_FAR)
        return jnp.roll(jnp.stack([piece, above, far, below]), y, axis=0)

    out_rows = lax.all_to_all(
        all_heads(pair[:, 384:]).reshape(16, 64, 128),
        "dp",
        split_axis=0,
        concat_axis=0,
        tiled=True,
    )
    grad_out = out_rows.transpose(1, 0, 2).reshape(64, D).astype(F32)
    in_rows = all_heads(pair[:, :384]).reshape(HEADS, 3, HD, 128)

    def rows_of(which):
        return in_rows[:, which].transpose(2, 0, 1).reshape(128, 1024).astype(F32)

    input_one = (stream_one.astype(F32) - mixed[None].astype(F32)).astype(BF)
    grad_two = (cotan_two.astype(F32) + change[None].astype(F32)).astype(BF)
    return (input_one, grad_two, rows_of(0), rows_of(1), rows_of(2), grad_out)


def solution(mesh):
    tokens, rows = P("dp", "seq", None), P("dp", None)
    return jax.shard_map(
        local,
        mesh=mesh,
        in_specs=(tokens,) * 4 + (rows,) * 5,
        out_specs=(tokens, tokens, rows, rows, rows, rows),
        check_vma=False,
    )
```

```python
import jax
import jax.numpy as jnp
from jax import lax
from jax.experimental import pallas as pl
from jax.experimental.pallas import tpu as pltpu
from jax.sharding import PartitionSpec as P

HEADS = 8
HD = 128
QBLK = 128
EPS = 1e-06
SCALE = HD ** (-0.5)
AXES = ("dp", "seq")
BF = jnp.bfloat16
F32 = jnp.float32
TB = 256
LEN = 2048
D = 2048

COORDS = [
    (z, xl, c, y, xh)
    for z in range(4)
    for xl in range(2)
    for c in range(2)
    for y in range(4)
    for xh in range(2)
]


def flat(z, xl, c, y, xh):
    return (z * 4 + xl * 2 + c) * 8 + y * 2 + xh


def perm(move):
    return [(flat(*at), flat(*move(*at))) for at in COORDS]


SWITCH = perm(lambda z, xl, c, y, xh: (z, 1 - xl, xh, y, c))
CROSS = perm(lambda z, xl, c, y, xh: (z, 1 - xl, xh, y, 1 - c))
CORE = perm(lambda z, xl, c, y, xh: (z, xl, 1 - c, y, xh))
Y_UP = perm(lambda z, xl, c, y, xh: (z, xl, c, (y + 1) % 4, xh))
Y_FAR = perm(lambda z, xl, c, y, xh: (z, xl, c, (y + 2) % 4, xh))
Y_DOWN = perm(lambda z, xl, c, y, xh: (z, xl, c, (y - 1) % 4, xh))
GROUP_YC = [
    [flat(z, xl, c, y, xh) for y in range(4) for c in range(2)]
    for z in range(4)
    for xl in range(2)
    for xh in range(2)
]
GROUP_ZX = [
    [flat(z, 1 - xl, c, y, xh) for z in range(4) for xl in range(2) for xh in range(2)]
    for y in range(4)
    for c in range(2)
]


def send(value, pairs):
    return lax.ppermute(value, AXES, pairs)


def ring_first(piece, up, down):
    return send(piece, up), send(piece, down)


def ring_second(below, above, up, down):
    half = below.shape[0] // 2
    return send(below[:half], up), send(above[half:], down)


def after(values, *earlier):
    return lax.optimization_barrier((tuple(values), earlier))[0]


STEPS = (0, -1, 1, 2)
SIZES = (TB, TB, TB, TB // 2, TB // 2) * 2


def dot(a, b, dims=((1,), (0,))):
    return lax.dot_general(a, b, (dims, ((), ())), preferred_element_type=F32)


NT = ((1,), (1,))
VM = pl.BlockSpec(memory_space=pltpu.VMEM)
SM = pl.BlockSpec(memory_space=pltpu.SMEM)


def call(kernel, outs, ins, scratch=(), flops=0, nbytes=0, smem=1):
    return pl.pallas_call(
        kernel,
        out_shape=outs,
        in_specs=[SM] * smem + [VM] * (len(ins) - smem),
        out_specs=jax.tree.map(lambda _: VM, outs),
        scratch_shapes=list(scratch),
        compiler_params=pltpu.CompilerParams(vmem_limit_bytes=28 * 2**20),
        cost_estimate=pl.CostEstimate(flops=flops, bytes_accessed=nbytes, transcendentals=0),
    )(*ins)


def norm_rows(values):
    values = values.astype(F32)
    inverse = lax.rsqrt(jnp.mean(values * values, axis=-1, keepdims=True) + EPS)
    return values * inverse, inverse


def normed_kernel(stream, out):
    out[...] = norm_rows(stream[...])[0].astype(BF)


def out_kernel(gathered, cotan, full, grad):
    for h in range(HEADS):
        for part in range(2):
            at = (2 * h + part) * 128
            rows = slice(h * HD + part * 64, h * HD + part * 64 + 64)
            full[rows, 0:1024] = gathered[at : at + 64, :]
            full[rows, 1024:D] = gathered[at + 64 : at + 128, :]
    for h in range(0, HEADS, 2):
        product = dot(cotan[...], full[h * HD : (h + 2) * HD, :], NT).astype(BF)
        grad[h] = product[:, :HD]
        grad[h + 1] = product[:, HD:]


def project_kernel(place, *refs):
    parts, (query, key, value, out, held, weight, sems) = refs[:10], refs[10:]
    copies, at = [], 0
    for slot, (part, size) in enumerate(zip(parts, SIZES)):
        copies.append(
            pltpu.make_async_copy(part, held.at[pl.ds(at, size), :], sems.at[slot])
        )
        at += size
    for copy in copies:
        copy.start()
    column = pl.multiple_of(place[8], 128)
    for which, source in enumerate((query, key, value)):
        weight[:, which * HD : (which + 1) * HD] = source[:, pl.ds(column, HD)]
    for side in range(2):
        for step in range(4):
            copies[side * 5 + step].wait()
            if step == 3:
                copies[side * 5 + 4].wait()
            slot = side * 4 + step
            at = pl.multiple_of(place[slot], TB)
            out[pl.ds(at, TB), :] = dot(
                held[slot * TB : (slot + 1) * TB, :], weight[...]
            ).astype(BF)


def attention_kernel(first, qkv, grad, out, turned, key_t, value_t, key_sum, value_sum):
    key_t[...] = qkv[:, 128:256].T
    value_t[...] = qkv[:, 256:384].T
    key_sum[...] = jnp.zeros_like(key_sum)
    value_sum[...] = jnp.zeros_like(value_sum)
    for block in range(LEN // TB):
        count = (block + 1) * TB
        rows = slice(block * TB, count)
        query = qkv[rows, 0:128]
        grad_rows = grad[rows, :]
        grad_t = grad_rows.T
        scores = dot(qkv[:count, 128:256], query.T)
        key_at = lax.broadcasted_iota(jnp.int32, (count, TB), 0)
        lane = lax.broadcasted_iota(jnp.int32, (1, TB), 1)
        earliest = jnp.where(lane < QBLK, first[0, 2 * block], first[0, 2 * block + 1])
        visible = (key_at >= earliest) & (key_at <= lane + block * TB)
        scores = jnp.where(visible, scores * SCALE, -1e30)
        top = jnp.max(scores, axis=0, keepdims=True)
        raised = jnp.exp(scores - top)
        probs = raised * (1.0 / jnp.sum(raised, axis=0, keepdims=True))
        probs_low = probs.astype(BF)
        attended = dot(value_t[:, :count], probs_low).astype(BF)
        row_dots = jnp.sum(
            grad_t.astype(F32) * attended.astype(F32), axis=0, keepdims=True
        )
        grad_probs = dot(qkv[:count, 256:384], grad_t)
        score_grad = (probs * (grad_probs - row_dots)).astype(BF)
        query_grad = (dot(key_t[:, :count], score_grad) * SCALE).astype(BF)
        key_sum[:count, :] += dot(score_grad, query)
        value_sum[:count, :] += dot(probs_low, grad_rows)
        out[rows, 0:128] = attended.T
        out[rows, 128:256] = query_grad.T
        turned[0:128, rows] = query_grad
        turned[384:512, rows] = attended
    key_grad = (key_sum[...] * SCALE).astype(BF)
    value_grad = value_sum[...].astype(BF)
    out[:, 256:384] = key_grad
    out[:, 384:512] = value_grad
    turned[128:256, :] = key_grad.T
    turned[256:384, :] = value_grad.T


def terms_kernel(place, turned, *refs):
    normed, cotan, out, ordered = refs[:10], refs[10:20], refs[20], refs[21]

    @pl.when(pl.program_id(0) == 0)
    def _():
        for slot in range(8):
            at = pl.multiple_of(place[slot], TB)
            ordered[:, slot * TB : (slot + 1) * TB] = turned[:, pl.ds(at, TB)]

    for low, high, tokens in ((0, 384, normed), (384, 512, cotan)):
        rows = jnp.concatenate([piece[...] for piece in tokens], axis=0)
        total = dot(ordered[low:high, :], rows)
        total = total.astype(BF)
        for part in range(4):
            out[part, low:high, :] = total[:, part * 128 : (part + 1) * 128]


def stream_kernel(
    place, stream, heads0, heads1, heads2, heads3, w_in, w_out, out_one, out_two, total, grads
):
    step = pl.program_id(0)

    @pl.when(step == 0)
    def _():
        for group, heads in enumerate((heads0, heads1, heads2, heads3)):
            for side in range(2):
                at = pl.multiple_of(place[9 + group * 2 + side], HD)
                for which in range(4):
                    grads[which, :, pl.ds(at, HD)] = heads[side, :, which * HD : (which + 1) * HD]

    part = dot(grads[1], w_in[:, 0:1024], NT)
    part = part + dot(grads[2], w_in[:, 1024:2048], NT)
    part = part + dot(grads[3], w_in[:, 2048:3072], NT)
    columns = pl.ds(pl.multiple_of(step * 512, 512), 512)
    total[:, columns] = part
    out_one[:, columns] = dot(grads[0], w_out[...]).astype(BF)

    @pl.when(step == 3)
    def _():
        normed, inverse = norm_rows(stream[...])
        grad = total[...]
        correction = jnp.mean(grad * normed, axis=-1, keepdims=True)
        out_two[...] = (inverse * (grad - normed * correction)).astype(BF)


def shape(dims, kind=BF):
    return jax.ShapeDtypeStruct(dims, kind)


def local(stream_one, stream_two, cotan_one, cotan_two, first_key, w_query, w_key, w_value, w_out):
    dp, seq = lax.axis_index("dp"), lax.axis_index("seq")
    core, y = dp % 2, seq // 2

    token_at = []
    for side in range(2):
        for step in STEPS:
            where = 2 * ((y + step) % 4) + (core if side == 0 else 1 - core)
            token_at.append(where * TB)
    head_at = [
        (2 * ((y + step) % 4) + (core if side == 0 else 1 - core)) * HD
        for step in STEPS
        for side in range(2)
    ]
    place = jnp.stack(token_at + [core * HD] + head_at).astype(jnp.int32)

    two = send(stream_two[0], SWITCH)
    first = send(first_key, SWITCH)
    (cot,) = after([cotan_one[0]], two)
    cot = send(cot, SWITCH)

    normed = call(normed_kernel, shape((TB, D)), [two], smem=0, nbytes=2 * TB * D * 2)
    below, above = ring_first(normed, Y_UP, Y_DOWN)
    far = after(ring_second(below, above, Y_UP, Y_DOWN), cot)
    normed_pieces = [normed, below, above, *far]
    normed_pieces = normed_pieces + [send(piece, CORE) for piece in normed_pieces]

    slim = jnp.concatenate(
        [jnp.concatenate([w_out[:, :1024], w_out[:, 1024:]], axis=0)]
        + [lax.dynamic_slice_in_dim(w, y * 256, 256, axis=1) for w in (w_query, w_key, w_value)],
        axis=1,
    )
    slim = lax.all_gather(slim, "dp", axis=0, tiled=True)
    w_query, w_key, w_value, _ = lax.optimization_barrier((w_query, w_key, w_value, normed))
    full_in = lax.all_gather(
        jnp.concatenate([w_query, w_key, w_value], axis=1), "dp", axis=0, tiled=True
    )

    full_out, by_head = pl.pallas_call(
        out_kernel,
        out_shape=(shape((1024, D)), shape((HEADS, TB, HD))),
        grid=(1,),
        in_specs=[
            pl.BlockSpec((D, 1024), lambda i: (0, 0)),
            pl.BlockSpec((TB, D), lambda i: (0, 0)),
        ],
        out_specs=(
            pl.BlockSpec((1024, D), lambda i: (0, 0)),
            pl.BlockSpec((HEADS, TB, HD), lambda i: (0, 0, 0)),
        ),
        compiler_params=pltpu.CompilerParams(vmem_limit_bytes=56 * 2**20),
        cost_estimate=pl.CostEstimate(
            flops=6 * 10**9, bytes_accessed=9 * 2**20, transcendentals=0
        ),
    )(slim, cot)
    grad = lax.all_to_all(
        by_head, AXES, split_axis=0, concat_axis=0, tiled=True, axis_index_groups=GROUP_YC
    ).reshape(LEN, HD)

    (cot_first,) = after([cot], far[1], slim)
    cot_below, cot_above = ring_first(cot_first, Y_UP, Y_DOWN)
    columns = [pl.BlockSpec((D, 256), lambda i, which=which: (0, 4 + which)) for which in range(3)]
    qkv = pl.pallas_call(
        project_kernel,
        out_shape=shape((LEN, 384)),
        grid=(1,),
        in_specs=[SM] + [pl.BlockSpec(memory_space=pl.ANY)] * 10 + columns,
        out_specs=pl.BlockSpec((LEN, 384), lambda i: (0, 0)),
        scratch_shapes=[
            pltpu.VMEM((LEN, D), BF),
            pltpu.VMEM((D, 384), BF),
            pltpu.SemaphoreType.DMA((10,)),
        ],
        compiler_params=pltpu.CompilerParams(vmem_limit_bytes=56 * 2**20),
        cost_estimate=pl.CostEstimate(
            flops=9 * 10**9, bytes_accessed=13 * 2**20, transcendentals=0
        ),
    )(place, *normed_pieces, slim, slim, slim)
    cot_below, cot_above = after([cot_below, cot_above], grad, qkv)
    cot_far = ring_second(cot_below, cot_above, Y_UP, Y_DOWN)
    cot_near = [cot, cot_below, cot_above]
    cot_swapped = [send(piece, CORE) for piece in cot_near]
    (qkv,) = after([qkv], *cot_swapped)
    by_position, turned = call(
        attention_kernel,
        (shape((LEN, 512)), shape((512, LEN))),
        [first, qkv, grad],
        scratch=[
            pltpu.VMEM((HD, LEN), BF),
            pltpu.VMEM((HD, LEN), BF),
            pltpu.VMEM((LEN, HD), F32),
            pltpu.VMEM((LEN, HD), F32),
        ],
        flops=20 * 10**9,
        nbytes=8 * 2**20,
    )

    blocks = by_position.reshape(4, 2, TB, 512)
    mine = lax.dynamic_index_in_dim(blocks, core, axis=1, keepdims=False)
    theirs = send(lax.dynamic_index_in_dim(blocks, 1 - core, axis=1, keepdims=False), CORE)
    def block_for(step):
        return jnp.stack(
            [
                lax.dynamic_index_in_dim(values, (y + step) % 4, axis=0, keepdims=False)
                for values in (mine, theirs)
            ]
        )

    heads = [
        block_for(0),
        send(block_for(1), Y_UP),
        send(block_for(-1), Y_DOWN),
        send(block_for(2), Y_FAR),
    ]
    cot_last = [send(piece, CORE) for piece in after(cot_far, turned)]
    cot_pieces = [*cot_near, *cot_far, *cot_swapped, *cot_last]

    wide = [pl.BlockSpec((size, 512), lambda i: (0, i)) for size in SIZES]
    terms = pl.pallas_call(
        terms_kernel,
        out_shape=shape((16, 512, 128)),
        grid=(4,),
        in_specs=[SM, pl.BlockSpec((512, LEN), lambda i: (0, 0))] + wide * 2,
        out_specs=pl.BlockSpec((4, 512, 128), lambda i: (i, 0, 0)),
        scratch_shapes=[pltpu.VMEM((512, LEN), BF)],
        compiler_params=pltpu.CompilerParams(vmem_limit_bytes=26 * 2**20),
        cost_estimate=pl.CostEstimate(
            flops=12 * 10**9, bytes_accessed=20 * 2**20, transcendentals=0
        ),
    )(place, turned, *normed_pieces, *cot_pieces)
    (terms,) = after([terms], heads[3])
    spread = lax.all_to_all(
        terms, AXES, split_axis=0, concat_axis=0, tiled=True, axis_index_groups=GROUP_ZX
    )
    rows_spec = pl.BlockSpec((TB, D), lambda i: (0, 0))
    mixed, change = pl.pallas_call(
        stream_kernel,
        out_shape=(shape((TB, D)), shape((TB, D))),
        grid=(4,),
        in_specs=[SM]
        + [rows_spec]
        + [pl.BlockSpec((2, TB, 512), lambda i: (0, 0, 0))] * 4
        + [pl.BlockSpec((512, 3072), lambda i: (i, 0))]
        + [pl.BlockSpec((1024, 512), lambda i: (0, i))],
        out_specs=(rows_spec, rows_spec),
        scratch_shapes=[pltpu.VMEM((TB, D), F32), pltpu.VMEM((4, TB, 1024), BF)],
        compiler_params=pltpu.CompilerParams(vmem_limit_bytes=56 * 2**20),
        cost_estimate=pl.CostEstimate(
            flops=14 * 10**9, bytes_accessed=22 * 2**20, transcendentals=0
        ),
    )(place, two, *heads, full_in, full_out)
    (spread,) = after([spread], mixed, change)
    summed = jnp.sum(spread.astype(F32), axis=0).astype(BF)
    near, cross = send(summed, SWITCH), send(summed, CROSS)
    mixed = send(mixed, SWITCH)
    near, cross = after([near, cross], mixed)
    (change,) = after([change], near, cross)
    change = send(change, SWITCH)
    x_zero = seq % 2 == 0
    pair = jnp.where(x_zero, jnp.stack([near, cross]), jnp.stack([cross, near]))

    def all_heads(piece):
        below, above, far = send(piece, Y_UP), send(piece, Y_DOWN), send(piece, Y_FAR)
        return jnp.roll(jnp.stack([piece, above, far, below]), y, axis=0)

    out_rows = lax.all_to_all(
        all_heads(pair[:, 384:]).reshape(16, 64, 128),
        "dp",
        split_axis=0,
        concat_axis=0,
        tiled=True,
    )
    grad_out = out_rows.transpose(1, 0, 2).reshape(64, D).astype(F32)
    in_rows = all_heads(pair[:, :384]).reshape(HEADS, 3, HD, 128)

    def rows_of(which):
        return in_rows[:, which].transpose(2, 0, 1).reshape(128, 1024).astype(F32)

    input_one = (stream_one.astype(F32) - mixed[None].astype(F32)).astype(BF)
    grad_two = (cotan_two.astype(F32) + change[None].astype(F32)).astype(BF)
    return (input_one, grad_two, rows_of(0), rows_of(1), rows_of(2), grad_out)


def solution(mesh):
    tokens, rows = P("dp", "seq", None), P("dp", None)
    return jax.shard_map(
        local,
        mesh=mesh,
        in_specs=(tokens,) * 4 + (rows,) * 5,
        out_specs=(tokens, tokens, rows, rows, rows, rows),
        check_vma=False,
    )
```
